512 devices in a mesh: gx: 32 (over y, z_lo), gy: 16 (over x, z_hi, core).
Axes of the slice: x: 4, y: 8, z: 8 (z_hi: 2, z_lo: 4; z = z_hi * 4 + z_lo), core: 2. Of those that a mesh axis runs over, the one named last changes fastest.
Arguments:
- density: bfloat16 [32, 32, 8, 128, 128], P('gx', 'gy'), may hold values from -0.09375 to 0.09375
- intersection: bfloat16 [32, 32, 8, 128, 128], P('gx', 'gy'), may hold values from -6 to 6
- columns: int32 [32, 32, 8], P('gx', 'gy'), may hold values from 0 to 1023, as said below
- counts: int32 [32, 32], P('gx', 'gy'), may hold values from 4 to 8, as said below
Outputs:
- purified: float32 [32, 32, 8, 128, 128], P('gx', 'gy')
The draws below stay inside these ranges and needn't reach their ends.
Inputs may be any that keep to these rules, and one draw needn't show every extreme that they name: `columns`: the first counts entries of a row are distinct block rows at most one step away from it in each grid direction, one of them the row itself; later entries are further such rows or the row itself. `counts`: rows at grid corners have 4, and the interior row (1, 1) has 8.
All inputs are finite; a program needn't handle non-finite values.
Results may differ from the reference program's by a relative error of at most 0.0049.
Values may be sent and summed in bfloat16 or wider, within the bound.
A program may use at most 64 MiB of HBM per device.

```python
import jax
import jax.numpy as jnp
from jax import lax

BS = 128
NB = 8
GXR = 32
GYR = 32


def pattern_draw(key):
    step_x = jnp.array([-1, -1, -1, 0, 0, 0, 1, 1, 1], jnp.int32)
    step_y = jnp.array([-1, 0, 1, -1, 0, 1, -1, 0, 1], jnp.int32)
    row_x = jnp.arange(GXR, dtype=jnp.int32)[:, None, None]
    row_y = jnp.arange(GYR, dtype=jnp.int32)[None, :, None]
    near_x = row_x + step_x
    near_y = row_y + step_y
    inside = (near_x >= 0) & (near_x < GXR) & (near_y >= 0) & (near_y < GYR)
    offset = jnp.arange(9, dtype=jnp.int32)
    scores = jax.random.randint(key, (GXR, GYR, 9), 0, 1000) * 16 + offset
    scores = jnp.where(offset == 4, 100000, scores)
    scores = jnp.where(inside, scores, offset - 100)
    order = jnp.argsort(-scores, axis=-1, stable=True)[..., :NB]
    ident = near_x * GYR + near_y
    own = row_x * GYR + row_y + jnp.zeros_like(ident)
    ident = jnp.where(inside, ident, own)
    chosen = jnp.take_along_axis(ident, order, axis=-1).astype(jnp.int32)
    avail = jnp.sum(inside.astype(jnp.int32), axis=-1)
    wanted = jax.random.randint(jax.random.fold_in(key, 7), (GXR, GYR), 5, NB + 1)
    middle = (row_x[:, :, 0] == 1) & (row_y[:, :, 0] == 1)
    wanted = jnp.where(middle, NB, wanted)
    return (chosen, jnp.minimum(wanted, avail).astype(jnp.int32))


def draw_columns(key, part):
    chosen, number = pattern_draw(key)
    return chosen


def draw_counts(key, part):
    chosen, number = pattern_draw(key)
    return number


def level_of(key, shape, split, low, high):
    gain = 1.0
    for dim, parts in split:
        draws = jax.random.uniform(jax.random.fold_in(jax.random.fold_in(key, 6), dim), (parts,), jnp.float32, low / len(split), high / len(split))
        gain = gain * jnp.repeat(jnp.exp(draws), shape[dim] // parts).reshape((-1,) + (1,) * (len(shape) - 1 - dim))
    return gain


def noise(rng, extent, spread, limit, pieces=(), kind=jnp.bfloat16):
    values = spread * jax.random.normal(rng, extent, jnp.float32)
    if pieces:
        values = values * level_of(rng, extent, pieces, -0.22, 0.18)
    return jnp.clip(values, -limit, limit).astype(kind)


def setup_inputs(seed: int = 0) -> dict:
    seeds = jax.random.split(jax.random.key(seed), 5)
    return {
        "density": noise(seeds[0], (GXR, GYR, NB, BS, BS), (NB * BS * 4) ** -0.5, 0.09375, ((0, 32), (1, 16))),
        "intersection": noise(seeds[1], (GXR, GYR, NB, BS, BS), 1.0, 6.0, ((0, 32), (1, 16))),
        "columns": draw_columns(jax.random.fold_in(seeds[4], 71), 0),
        "counts": draw_counts(jax.random.fold_in(seeds[4], 71), 0),
    }


def trunc_mult(left, right, pattern):
    total = GXR * GYR
    left_f = left.reshape(total, NB, BS, BS)
    right_f = right.reshape(total, NB, BS, BS)
    pat_f = pattern.reshape(total, NB)

    def one_row(row):
        cols = pat_f[row]
        live = cols >= 0
        neighbor = jnp.where(live, cols, row).astype(jnp.int32)
        gathered = right_f[neighbor]
        their = pat_f[neighbor]
        match = (their[:, :, None] == cols[None, None, :]) & live[None, None, :] & live[:, None, None]
        chosen = jnp.einsum("kbc,kbxy->kcxy", match.astype(jnp.float32), gathered.astype(jnp.float32))
        return jnp.einsum("kxy,kcyz->cxz", left_f[row].astype(jnp.float32), chosen)

    result = lax.map(one_row, jnp.arange(total, dtype=jnp.int32))
    return result.reshape(GXR, GYR, NB, BS, BS)


def reference(density, intersection, columns, counts):
    slots = jnp.arange(NB, dtype=jnp.int32)
    pattern = jnp.where(slots[None, None, :] < counts[:, :, None], columns, -1).astype(jnp.int32)
    lsprod = trunc_mult(density, intersection, pattern).astype(jnp.bfloat16)
    lslprod = trunc_mult(lsprod, density, pattern).astype(jnp.bfloat16)
    quintic = trunc_mult(lsprod, lslprod, pattern)
    return 3.0 * lslprod.astype(jnp.float32) - 2.0 * quintic
```

```python
import functools

import jax
import jax.numpy as jnp
from jax import lax
from jax.experimental import pallas as pl
from jax.experimental.pallas import tpu as pltpu
from jax.sharding import PartitionSpec as P

MESH = pl.DeviceIdType.MESH
BF16 = jnp.bfloat16
F32 = jnp.float32
STEPS = (-1, 0, 1)


def kernel(
    size_x, size_y, slots, l_hbm, s_hbm, cols, cnts, k_out,
    offs_out, offs, raw_s, raw_l, bs, bl, bq, ls, kst, kret,
    t_send, t_recv, o_send, o_recv, h_send, h_recv, k_send, k_recv,
):
    gx = lax.axis_index("gx")
    gy = lax.axis_index("gy")
    y, r = gx // 4, gx % 4
    x, h, k = gy // 4, (gy // 2) % 2, gy % 2
    z = 4 * h + r

    def dev(x_, y_, z_, k_):
        return (y_ * 4 + z_ % 4, (x_ * 2 + z_ // 4) * 2 + k_)

    keeps = r // 2 == k
    at_slot = r % 2
    to = [dev(x, y, 4 * h + 2 * k + j, r // 2) for j in range(2)]
    home = [dev(x, y, 4 * h + 2 * k + q, r // 2) for q in range(2)]
    home_row = r % 2
    stays = [jnp.logical_and(keeps, at_slot == j) for j in range(2)]

    up_z = z + 1
    z_next = dev((x + up_z // 8) % size_x, y, up_z % 8, k)
    dn_z = z + 7
    z_prev = dev((x + size_x - 1 + dn_z // 8) % size_x, y, dn_z % 8, k)
    x_next = dev(x, (y + k) % size_y, z, 1 - k)
    x_prev = dev(x, (y + size_y - 1 + k) % size_y, z, 1 - k)

    barrier = pltpu.get_barrier_semaphore()
    for d in (z_next, z_prev, x_next, x_prev):
        pl.semaphore_signal(barrier, inc=1, device_id=d, device_id_type=MESH)
    for j in range(2):
        @pl.when(jnp.logical_not(stays[j]))
        def _():
            pl.semaphore_signal(barrier, inc=1, device_id=to[j], device_id_type=MESH)
            pl.semaphore_signal(barrier, inc=1, device_id=home[j], device_id_type=MESH)

    grid_y = 8 * size_x
    for j in range(2):
        for b in range(slots):
            col = cols[0, j, b]
            dx = col // grid_y - gx
            dy = col % grid_y - (2 * gy + j)
            offs_out[j, b] = jnp.where(b < cnts[0, j], (dy + 1) * 3 + dx + 1, 9)

    zero = jnp.zeros((128, 128), BF16)
    for q in range(2):
        raw_s[q, slots] = zero
        raw_l[q, slots] = zero
        kst[q, 9] = zero

    pl.semaphore_wait(barrier, jnp.where(keeps, 6, 8))

    def send(src, dst, j, ssem, rsem, d):
        return pltpu.make_async_remote_copy(
            src_ref=src, dst_ref=dst, send_sem=ssem, recv_sem=rsem,
            device_id=d, device_id_type=MESH,
        )

    def arrive(dst, sem):
        pltpu.make_async_copy(dst, dst, sem).wait()

    live = pl.ds(0, slots)
    outs = []

    def route(src, dst, ssem, rsem, j, d):
        cp = send(src, dst, j, ssem, rsem, d)

        @pl.when(jnp.logical_not(stays[j]))
        def _():
            cp.start()

        @pl.when(stays[j])
        def _():
            pltpu.make_async_copy(src, dst, rsem).start()

        outs.append((cp, j))

    for j in range(2):
        route(offs_out.at[j], offs.at[at_slot], o_send.at[j], o_recv.at[at_slot], j, to[j])
    for m, (src, raw) in enumerate(((s_hbm, raw_s), (l_hbm, raw_l))):
        for j in range(2):
            route(
                src.at[0, j], raw.at[at_slot, live],
                t_send.at[m, j], t_recv.at[m, at_slot], j, to[j],
            )

    for q in range(2):
        arrive(offs.at[q], o_recv.at[q])
    place = []
    for q in range(2):
        mine = [offs[q, b] for b in range(slots)]
        row = []
        for d in range(9):
            s = jnp.int32(slots)
            for b in range(slots):
                s = jnp.where(mine[b] == d, b, s)
            row.append(s)
        place.append(row)

    def spread(m, raw, out):
        for q in range(2):
            arrive(raw.at[q, live], t_recv.at[m, q])
        for q in range(2):
            for d in range(9):
                out[1 + q, 1, d // 3, d % 3] = raw[q, place[q][d]]

    def side(m, b):
        c = []
        for n, (src, dst, d) in enumerate((
            (b.at[pl.ds(1, 2), 1, pl.ds(1, 2)], b.at[pl.ds(1, 2), 0, pl.ds(1, 2)], z_next),
            (b.at[pl.ds(1, 2), 1, pl.ds(0, 2)], b.at[pl.ds(1, 2), 2, pl.ds(0, 2)], z_prev),
            (b.at[2, 1, :, pl.ds(1, 2)], b.at[0, 1, :, pl.ds(1, 2)], x_next),
            (b.at[1, 1, :, pl.ds(0, 2)], b.at[3, 1, :, pl.ds(0, 2)], x_prev),
        )):
            cp = send(src, dst, 0, h_send.at[m, n], h_recv.at[m, n], d)
            cp.start()
            c.append(cp)
        return c

    def corners(m, b, c):
        c[0].wait_recv()
        c[1].wait_recv()
        n = 4
        for ny, dys in ((0, pl.ds(1, 2)), (2, pl.ds(0, 2))):
            for src, dst, dxs, d in ((2, 0, pl.ds(1, 2), x_next), (1, 3, pl.ds(0, 2), x_prev)):
                cp = send(
                    b.at[src, ny, dys, dxs], b.at[dst, ny, dys, dxs],
                    0, h_send.at[m, n], h_recv.at[m, n], d,
                )
                cp.start()
                c.append(cp)
                n += 1

    def joined(c):
        for cp in c[2:]:
            cp.wait_recv()

    def cell(a, b, q, cy, cx):
        near = [
            (ny, nx) for ny in STEPS for nx in STEPS
            if abs(cy - ny) <= 1 and abs(cx - nx) <= 1
        ]
        lhs = jnp.concatenate([a(q, ny, nx) for ny, nx in near], axis=1)
        rhs = jnp.concatenate(
            [b[1 + q + nx, 1 + ny, cy - ny + 1, cx - nx + 1] for ny, nx in near], axis=0
        )
        return jnp.dot(lhs, rhs, preferred_element_type=F32)

    def trunc(value, q, d):
        return jnp.where(place[q][d] < slots, value, 0.0).astype(BF16)

    spread(0, raw_s, bs)
    c_s = side(0, bs)
    spread(1, raw_l, bl)
    c_l = side(1, bl)
    corners(0, bs, c_s)
    joined(c_s)

    def left_l(q, ny, nx):
        return bl[1 + q, 1, ny + 1, nx + 1]

    def left_ls(q, ny, nx):
        return ls[q, (ny + 1) * 3 + nx + 1]

    for q in range(2):
        for cy in STEPS:
            for cx in STEPS:
                d = (cy + 1) * 3 + cx + 1
                ls[q, d] = trunc(cell(left_l, bs, q, cy, cx), q, d)
    corners(1, bl, c_l)
    joined(c_l)
    for q in range(2):
        for cy in STEPS:
            for cx in STEPS:
                d = (cy + 1) * 3 + cx + 1
                bq[1 + q, 1, cy + 1, cx + 1] = trunc(cell(left_ls, bl, q, cy, cx), q, d)
    c_q = side(2, bq)
    corners(2, bq, c_q)
    joined(c_q)
    backs = []
    for q in range(2):
        for cy in STEPS:
            for cx in STEPS:
                d = (cy + 1) * 3 + cx + 1
                lsl = bq[1 + q, 1, cy + 1, cx + 1].astype(F32)
                kst[q, d] = (3.0 * lsl - 2.0 * cell(left_ls, bq, q, cy, cx)).astype(BF16)
        for b in range(slots):
            kret[q, b] = kst[q, offs[q, b]]
        cp = send(
            kret.at[q], k_out.at[0, home_row], 0, k_send.at[q], k_recv.at[home_row], home[q]
        )

        @pl.when(jnp.logical_not(stays[q]))
        def _():
            cp.start()

        @pl.when(stays[q])
        def _():
            pltpu.make_async_copy(kret.at[q], k_out.at[0, home_row], k_recv.at[home_row]).start()

        outs.append((cp, q))

    for c in (c_s, c_l, c_q):
        for cp in c:
            cp.wait_send()
    for cp, j in outs:
        @pl.when(jnp.logical_not(stays[j]))
        def _():
            cp.wait_send()
    for j in range(2):
        arrive(k_out.at[0, j], k_recv.at[j])


def on_device(density, intersection, columns, counts):
    size_y = lax.axis_size("gx") // 4
    size_x = lax.axis_size("gy") // 4
    slots = columns.shape[-1]
    block = (128, 128)
    dma = pltpu.SemaphoreType.DMA
    purified = pl.pallas_call(
        functools.partial(kernel, size_x, size_y, slots),
        out_shape=jax.ShapeDtypeStruct(density.shape, BF16),
        in_specs=[
            pl.BlockSpec(memory_space=pl.ANY),
            pl.BlockSpec(memory_space=pl.ANY),
            pl.BlockSpec(memory_space=pltpu.SMEM),
            pl.BlockSpec(memory_space=pltpu.SMEM),
        ],
        out_specs=pl.BlockSpec(memory_space=pl.ANY),
        scratch_shapes=[
            pltpu.SMEM((2, slots), jnp.int32),
            pltpu.SMEM((2, slots), jnp.int32),
            pltpu.VMEM((2, slots + 1) + block, BF16),
            pltpu.VMEM((2, slots + 1) + block, BF16),
            pltpu.VMEM((4, 3, 3, 3) + block, BF16),
            pltpu.VMEM((4, 3, 3, 3) + block, BF16),
            pltpu.VMEM((4, 3, 3, 3) + block, BF16),
            pltpu.VMEM((2, 9) + block, BF16),
            pltpu.VMEM((2, 10) + block, BF16),
            pltpu.VMEM((2, slots) + block, BF16),
            dma((2, 2)), dma((2, 2)),
            dma((2,)), dma((2,)),
            dma((3, 8)), dma((3, 8)),
            dma((2,)), dma((2,)),
        ],
        compiler_params=pltpu.CompilerParams(
            collective_id=0, has_side_effects=True, vmem_limit_bytes=40 << 20
        ),
        cost_estimate=pl.CostEstimate(
            flops=3 * 2 * 49 * 2 * 128**3, bytes_accessed=3 << 20, transcendentals=0
        ),
    )(density, intersection, columns, counts)
    return purified.astype(F32)


def solution(mesh):
    placed = (
        P("gx", "gy", None, None, None),
        P("gx", "gy", None, None, None),
        P("gx", "gy", None),
        P("gx", "gy"),
    )
    return jax.shard_map(
        on_device,
        mesh=mesh,
        in_specs=placed,
        out_specs=P("gx", "gy", None, None, None),
        check_vma=False,
    )
```

```python
import functools

import jax
import jax.numpy as jnp
from jax import lax
from jax.experimental import pallas as pl
from jax.experimental.pallas import tpu as pltpu
from jax.sharding import PartitionSpec as P

MESH = pl.DeviceIdType.MESH
BF16 = jnp.bfloat16
F32 = jnp.float32
STEPS = (-1, 0, 1)


def kernel(
    size_x, size_y, slots, l_hbm, s_hbm, cols_hbm, cnts_hbm, k_out,
    cols, cnts, arg_sem, offs_out, offs, raw_s, raw_l, bs, bl, bq, ls, kst, kret,
    t_send, t_recv, o_send, o_recv, h_send, h_recv, k_send, k_recv,
):
    gx = lax.axis_index("gx")
    gy = lax.axis_index("gy")
    y, r = gx // 4, gx % 4
    x, h, k = gy // 4, (gy // 2) % 2, gy % 2
    z = 4 * h + r

    def dev(x_, y_, z_, k_):
        return (y_ * 4 + z_ % 4, (x_ * 2 + z_ // 4) * 2 + k_)

    keeps = r // 2 == k
    at_slot = r % 2
    to = [dev(x, y, 4 * h + 2 * k + j, r // 2) for j in range(2)]
    home = [dev(x, y, 4 * h + 2 * k + q, r // 2) for q in range(2)]
    home_row = r % 2
    stays = [jnp.logical_and(keeps, at_slot == j) for j in range(2)]

    up_z = z + 1
    z_next = dev((x + up_z // 8) % size_x, y, up_z % 8, k)
    dn_z = z + 7
    z_prev = dev((x + size_x - 1 + dn_z // 8) % size_x, y, dn_z % 8, k)
    y_peer = dev(x, (y + size_y - 1 + 2 * k) % size_y, z, 1 - k)
    sibling = dev(x, y, z, 1 - k)
    q_out, q_in = k, 1 - k

    pattern_in = [
        pltpu.make_async_copy(cols_hbm, cols, arg_sem.at[0]),
        pltpu.make_async_copy(cnts_hbm, cnts, arg_sem.at[1]),
    ]
    for cp in pattern_in:
        cp.start()
    barrier = pltpu.get_barrier_semaphore()
    for d in (z_next, z_prev, y_peer, sibling):
        pl.semaphore_signal(barrier, inc=1, device_id=d, device_id_type=MESH)
    for j in range(2):
        @pl.when(jnp.logical_not(stays[j]))
        def _():
            pl.semaphore_signal(barrier, inc=1, device_id=to[j], device_id_type=MESH)
            pl.semaphore_signal(barrier, inc=1, device_id=home[j], device_id_type=MESH)

    for cp in pattern_in:
        cp.wait()
    grid_y = 8 * size_x
    for j in range(2):
        for b in range(slots):
            col = cols[0, j, b]
            dx = col // grid_y - gx
            dy = col % grid_y - (2 * gy + j)
            offs_out[j, b] = jnp.where(b < cnts[0, j], (dy + 1) * 3 + dx + 1, 9)

    zero = jnp.zeros((128, 128), BF16)
    for q in range(2):
        raw_s[q, slots] = zero
        raw_l[q, slots] = zero
        kst[q, 9] = zero

    pl.semaphore_wait(barrier, jnp.where(keeps, 6, 8))

    def send(src, dst, j, ssem, rsem, d):
        return pltpu.make_async_remote_copy(
            src_ref=src, dst_ref=dst, send_sem=ssem, recv_sem=rsem,
            device_id=d, device_id_type=MESH,
        )

    def arrive(dst, sem):
        pltpu.make_async_copy(dst, dst, sem).wait()

    live = pl.ds(0, slots)
    outs = []

    def route(src, dst, ssem, rsem, j, d):
        cp = send(src, dst, j, ssem, rsem, d)

        @pl.when(jnp.logical_not(stays[j]))
        def _():
            cp.start()

        @pl.when(stays[j])
        def _():
            pltpu.make_async_copy(src, dst, rsem).start()

        outs.append((cp, stays[j]))

    for j in range(2):
        route(offs_out.at[j], offs.at[at_slot], o_send.at[j], o_recv.at[at_slot], j, to[j])
    for m, (src, raw) in enumerate(((s_hbm, raw_s), (l_hbm, raw_l))):
        for j in range(2):
            route(
                src.at[0, j], raw.at[at_slot, live],
                t_send.at[m, j], t_recv.at[m, at_slot], j, to[j],
            )

    for q in range(2):
        arrive(offs.at[q], o_recv.at[q])
    place = []
    for q in range(2):
        mine = [offs[q, b] for b in range(slots)]
        row = []
        for d in range(9):
            s = jnp.int32(slots)
            for b in range(slots):
                s = jnp.where(mine[b] == d, b, s)
            row.append(s)
        place.append(row)

    def spread(m, raw, out):
        for q in range(2):
            arrive(raw.at[q, live], t_recv.at[m, q])
        for q in range(2):
            for d in range(9):
                out[1 + q, 1, d // 3, d % 3] = raw[q, place[q][d]]

    def halo(m, b, n, src, dst, d):
        cp = send(src, dst, 0, h_send.at[m, n], h_recv.at[m, n], d)
        cp.start()
        return cp

    def side_out(m, b):
        nx = 1 + q_out
        return [
            halo(m, b, 0, b.at[nx, 1, pl.ds(1, 2)], b.at[nx, 0, pl.ds(1, 2)], z_next),
            halo(m, b, 1, b.at[nx, 1, pl.ds(0, 2)], b.at[nx, 2, pl.ds(0, 2)], z_prev),
            halo(m, b, 2, b.at[nx, 1, :, pl.ds(k, 2)], b.at[3 - 3 * k, 1, :, pl.ds(k, 2)], y_peer),
        ]

    def side_in(m, b):
        nx = 1 + q_in
        return [
            halo(m, b, 5, b.at[nx, 1, pl.ds(1, 2)], b.at[nx, 0, pl.ds(1, 2)], z_next),
            halo(m, b, 6, b.at[nx, 1, pl.ds(0, 2)], b.at[nx, 2, pl.ds(0, 2)], z_prev),
            halo(m, b, 7, b.at[nx, 1, :, pl.ds(1 - k, 2)], b.at[3 * k, 1, :, pl.ds(1 - k, 2)], sibling),
        ]

    def corners_out(m, b, c):
        nx = 1 + q_out
        for n, (ny, dy) in enumerate(((0, 1), (2, 0))):
            c[n].wait_recv()
            c.append(halo(
                m, b, 3 + n, b.at[nx, ny, pl.ds(dy, 2), pl.ds(k, 2)],
                b.at[3 - 3 * k, ny, pl.ds(dy, 2), pl.ds(k, 2)], y_peer,
            ))

    def corners_in(m, b, c):
        nx = 1 + q_in
        for n, (ny, dy) in enumerate(((0, 1), (2, 0))):
            c[n].wait_recv()
            c.append(halo(
                m, b, 8 + n, b.at[nx, ny, pl.ds(dy, 2), pl.ds(1 - k, 2)],
                b.at[3 * k, ny, pl.ds(dy, 2), pl.ds(1 - k, 2)], sibling,
            ))

    def joined(c):
        for cp in c[2:]:
            cp.wait_recv()

    def cell(a, b, q, cy, cx):
        near = [
            (ny, nx) for ny in STEPS for nx in STEPS
            if abs(cy - ny) <= 1 and abs(cx - nx) <= 1
        ]
        lhs = jnp.concatenate([a(q, ny, nx) for ny, nx in near], axis=1)
        rhs = jnp.concatenate(
            [b[1 + q + nx, 1 + ny, cy - ny + 1, cx - nx + 1] for ny, nx in near], axis=0
        )
        return jnp.dot(lhs, rhs, preferred_element_type=F32)

    spread(0, raw_s, bs)
    c_s_out, c_s_in = side_out(0, bs), side_in(0, bs)
    spread(1, raw_l, bl)
    c_l_out, c_l_in = side_out(1, bl), side_in(1, bl)
    corners_out(0, bs, c_s_out)
    corners_in(0, bs, c_s_in)
    joined(c_s_out)
    joined(c_s_in)
    corners_out(1, bl, c_l_out)

    def left_l(q, ny, nx):
        return bl[1 + q, 1, ny + 1, nx + 1]

    def left_ls(q, ny, nx):
        return ls[q, (ny + 1) * 3 + nx + 1]

    def product(q, left, right, out):
        for d in range(9):
            dy, dx = d // 3, d % 3
            used = jnp.where(q == 0, place[0][d], place[1][d]) < slots
            value = cell(left, right, q, dy - 1, dx - 1)
            out(q, dy, dx, jnp.where(used, value, 0.0).astype(BF16))

    def put_ls(q, dy, dx, value):
        ls[q, dy * 3 + dx] = value

    def put_lsl(q, dy, dx, value):
        bq[1 + q, 1, dy, dx] = value

    product(q_out, left_l, bs, put_ls)
    product(q_in, left_l, bs, put_ls)
    corners_in(1, bl, c_l_in)
    joined(c_l_out)
    joined(c_l_in)
    product(q_out, left_ls, bl, put_lsl)
    c_q_out = side_out(2, bq)
    product(q_in, left_ls, bl, put_lsl)
    c_q_in = side_in(2, bq)
    corners_out(2, bq, c_q_out)
    corners_in(2, bq, c_q_in)
    joined(c_q_in)
    for n, q in enumerate((q_in, q_out)):
        if n == 1:
            joined(c_q_out)
        for d in range(9):
            dy, dx = d // 3, d % 3
            lsl = bq[1 + q, 1, dy, dx].astype(F32)
            kst[q, d] = (3.0 * lsl - 2.0 * cell(left_ls, bq, q, dy - 1, dx - 1)).astype(BF16)
        for b in range(slots):
            kret[q, b] = kst[q, offs[q, b]]
        there = dev(x, y, 4 * h + 2 * k + q, r // 2)
        stay = jnp.logical_and(keeps, at_slot == q)
        cp = send(
            kret.at[q], k_out.at[0, home_row], 0, k_send.at[n], k_recv.at[home_row], there
        )

        @pl.when(jnp.logical_not(stay))
        def _():
            cp.start()

        @pl.when(stay)
        def _():
            pltpu.make_async_copy(kret.at[q], k_out.at[0, home_row], k_recv.at[home_row]).start()

        outs.append((cp, stay))

    for c in (c_s_out, c_s_in, c_l_out, c_l_in, c_q_out, c_q_in):
        for cp in c:
            cp.wait_send()
    for cp, stay in outs:
        @pl.when(jnp.logical_not(stay))
        def _():
            cp.wait_send()
    for j in range(2):
        arrive(k_out.at[0, j], k_recv.at[j])


def on_device(density, intersection, columns, counts):
    size_y = lax.axis_size("gx") // 4
    size_x = lax.axis_size("gy") // 4
    slots = columns.shape[-1]
    block = (128, 128)
    dma = pltpu.SemaphoreType.DMA
    purified = pl.pallas_call(
        functools.partial(kernel, size_x, size_y, slots),
        out_shape=jax.ShapeDtypeStruct(density.shape, BF16),
        in_specs=[
            pl.BlockSpec(memory_space=pl.ANY),
            pl.BlockSpec(memory_space=pl.ANY),
            pl.BlockSpec(memory_space=pl.ANY),
            pl.BlockSpec(memory_space=pl.ANY),
        ],
        out_specs=pl.BlockSpec(memory_space=pl.ANY),
        scratch_shapes=[
            pltpu.SMEM(columns.shape, jnp.int32),
            pltpu.SMEM(counts.shape, jnp.int32),
            dma((2,)),
            pltpu.SMEM((2, slots), jnp.int32),
            pltpu.SMEM((2, slots), jnp.int32),
            pltpu.VMEM((2, slots + 1) + block, BF16),
            pltpu.VMEM((2, slots + 1) + block, BF16),
            pltpu.VMEM((4, 3, 3, 3) + block, BF16),
            pltpu.VMEM((4, 3, 3, 3) + block, BF16),
            pltpu.VMEM((4, 3, 3, 3) + block, BF16),
            pltpu.VMEM((2, 9) + block, BF16),
            pltpu.VMEM((2, 10) + block, BF16),
            pltpu.VMEM((2, slots) + block, BF16),
            dma((2, 2)), dma((2, 2)),
            dma((2,)), dma((2,)),
            dma((3, 10)), dma((3, 10)),
            dma((2,)), dma((2,)),
        ],
        compiler_params=pltpu.CompilerParams(
            collective_id=0, has_side_effects=True, vmem_limit_bytes=60 << 20
        ),
        cost_estimate=pl.CostEstimate(
            flops=3 * 2 * 49 * 2 * 128**3, bytes_accessed=3 << 20, transcendentals=0
        ),
    )(density, intersection, columns, counts)
    return purified.astype(F32)


def solution(mesh):
    placed = (
        P("gx", "gy", None, None, None),
        P("gx", "gy", None, None, None),
        P("gx", "gy", None),
        P("gx", "gy"),
    )
    return jax.shard_map(
        on_device,
        mesh=mesh,
        in_specs=placed,
        out_specs=P("gx", "gy", None, None, None),
        check_vma=False,
    )
```

```python
import functools

import jax
import jax.numpy as jnp
from jax import lax
from jax.experimental import pallas as pl
from jax.experimental.pallas import tpu as pltpu
from jax.sharding import PartitionSpec as P

MESH = pl.DeviceIdType.MESH
BF16 = jnp.bfloat16
F32 = jnp.float32
STEPS = (-1, 0, 1)


def kernel(
    size_x, size_y, slots, l_hbm, s_hbm, cols_hbm, cnts_hbm, k_out,
    cols, cnts, arg_sem, offs_out, offs, raw_s, raw_l, bs, bl, bq, ls, kst, kret,
    t_send, t_recv, o_send, o_recv, h_send, h_recv, k_send, k_recv,
):
    gx = lax.axis_index("gx")
    gy = lax.axis_index("gy")
    y, r = gx // 4, gx % 4
    x, h, k = gy // 4, (gy // 2) % 2, gy % 2
    z = 4 * h + r

    def dev(x_, y_, z_, k_):
        return (y_ * 4 + z_ % 4, (x_ * 2 + z_ // 4) * 2 + k_)

    keeps = r // 2 == k
    at_slot = r % 2
    to = [dev(x, y, 4 * h + 2 * k + j, r // 2) for j in range(2)]
    home = [dev(x, y, 4 * h + 2 * k + q, r // 2) for q in range(2)]
    home_row = r % 2
    stays = [jnp.logical_and(keeps, at_slot == j) for j in range(2)]

    up_z = z + 1
    z_next = dev((x + up_z // 8) % size_x, y, up_z % 8, k)
    dn_z = z + 7
    z_prev = dev((x + size_x - 1 + dn_z // 8) % size_x, y, dn_z % 8, k)
    y_peer = dev(x, (y + size_y - 1 + 2 * k) % size_y, z, 1 - k)
    sibling = dev(x, y, z, 1 - k)
    q_out, q_in = k, 1 - k
    has_next = jnp.logical_or(x < size_x - 1, z < 7)
    has_prev = jnp.logical_or(x > 0, z > 0)
    has_y = jnp.where(k == 0, y > 0, y < size_y - 1)

    pattern_in = [
        pltpu.make_async_copy(cols_hbm, cols, arg_sem.at[0]),
        pltpu.make_async_copy(cnts_hbm, cnts, arg_sem.at[1]),
    ]
    for cp in pattern_in:
        cp.start()
    barrier = pltpu.get_barrier_semaphore()
    pl.semaphore_signal(barrier, inc=1, device_id=sibling, device_id_type=MESH)
    for there, d in ((has_next, z_next), (has_prev, z_prev), (has_y, y_peer)):
        @pl.when(there)
        def _():
            pl.semaphore_signal(barrier, inc=1, device_id=d, device_id_type=MESH)

    for j in range(2):
        @pl.when(jnp.logical_not(stays[j]))
        def _():
            pl.semaphore_signal(barrier, inc=1, device_id=to[j], device_id_type=MESH)
            pl.semaphore_signal(barrier, inc=1, device_id=home[j], device_id_type=MESH)

    for cp in pattern_in:
        cp.wait()
    grid_y = 8 * size_x
    for j in range(2):
        for b in range(slots):
            col = cols[0, j, b]
            dx = col // grid_y - gx
            dy = col % grid_y - (2 * gy + j)
            offs_out[j, b] = jnp.where(b < cnts[0, j], (dy + 1) * 3 + dx + 1, 9)

    zero = jnp.zeros((128, 128), BF16)

    def blank(b, nx, ny):
        def cell_row(i, _):
            b[nx, ny, i // 3, i % 3] = zero
            return 0

        lax.fori_loop(0, 9, cell_row, 0)

    for b in (bs, bl, bq):
        @pl.when(jnp.logical_not(has_prev))
        def _():
            blank(b, 1, 0)
            blank(b, 2, 0)

        @pl.when(jnp.logical_not(has_next))
        def _():
            blank(b, 1, 2)
            blank(b, 2, 2)

        @pl.when(jnp.logical_not(has_y))
        def _():
            for ny in range(3):
                blank(b, 3 * k, ny)

    for q in range(2):
        raw_s[q, slots] = zero
        raw_l[q, slots] = zero
        kst[q, 9] = zero

    pl.semaphore_wait(
        barrier,
        jnp.where(keeps, 3, 5) + jnp.where(has_next, 1, 0) + jnp.where(has_prev, 1, 0)
        + jnp.where(has_y, 1, 0),
    )

    def send(src, dst, j, ssem, rsem, d):
        return pltpu.make_async_remote_copy(
            src_ref=src, dst_ref=dst, send_sem=ssem, recv_sem=rsem,
            device_id=d, device_id_type=MESH,
        )

    def arrive(dst, sem):
        pltpu.make_async_copy(dst, dst, sem).wait()

    live = pl.ds(0, slots)
    outs = []

    def route(src, dst, ssem, rsem, j, d):
        cp = send(src, dst, j, ssem, rsem, d)

        @pl.when(jnp.logical_not(stays[j]))
        def _():
            cp.start()

        @pl.when(stays[j])
        def _():
            pltpu.make_async_copy(src, dst, rsem).start()

        outs.append((cp, stays[j]))

    for j in range(2):
        route(offs_out.at[j], offs.at[at_slot], o_send.at[j], o_recv.at[at_slot], j, to[j])
    for m, (src, raw) in enumerate(((s_hbm, raw_s), (l_hbm, raw_l))):
        for j in (k, 1 - k):
            stay = jnp.logical_and(keeps, at_slot == j)
            there = dev(x, y, 4 * h + 2 * k + j, r // 2)
            cp = send(
                src.at[0, j], raw.at[at_slot, live], 0,
                t_send.at[m, j], t_recv.at[m, at_slot], there,
            )

            @pl.when(jnp.logical_not(stay))
            def _():
                cp.start()

            @pl.when(stay)
            def _():
                pltpu.make_async_copy(
                    src.at[0, j], raw.at[at_slot, live], t_recv.at[m, at_slot]
                ).start()

            outs.append((cp, stay))

    for q in range(2):
        arrive(offs.at[q], o_recv.at[q])
    place = []
    for q in range(2):
        mine = [offs[q, b] for b in range(slots)]
        row = []
        for d in range(9):
            s = jnp.int32(slots)
            for b in range(slots):
                s = jnp.where(mine[b] == d, b, s)
            row.append(s)
        place.append(row)

    def spread(m, raw, out):
        for q in range(2):
            arrive(raw.at[q, live], t_recv.at[m, q])
        for q in range(2):
            for d in range(9):
                out[1 + q, 1, d // 3, d % 3] = raw[q, place[q][d]]

    def halo(m, b, n, src, dst, d, sent=None, comes=None):
        cp = send(src, dst, 0, h_send.at[m, n], h_recv.at[m, n], d)
        if sent is None:
            cp.start()
        else:
            pl.when(sent)(cp.start)
        return cp, sent, comes

    def landed(c):
        cp, _, comes = c
        if comes is None:
            cp.wait_recv()
        else:
            pl.when(comes)(cp.wait_recv)

    def left(c):
        cp, sent, _ = c
        if sent is None:
            cp.wait_send()
        else:
            pl.when(sent)(cp.wait_send)

    def along_z(m, b, n, q):
        nx = 1 + q
        return [
            halo(
                m, b, n, b.at[nx, 1, pl.ds(1, 2)], b.at[nx, 0, pl.ds(1, 2)],
                z_next, has_next, has_prev,
            ),
            halo(
                m, b, n + 1, b.at[nx, 1, pl.ds(0, 2)], b.at[nx, 2, pl.ds(0, 2)],
                z_prev, has_prev, has_next,
            ),
        ]

    def side_out(m, b):
        return along_z(m, b, 0, q_out) + [halo(
            m, b, 2, b.at[1 + q_out, 1, :, pl.ds(k, 2)],
            b.at[3 - 3 * k, 1, :, pl.ds(k, 2)], y_peer, has_y, has_y,
        )]

    def side_in(m, b):
        return along_z(m, b, 5, q_in) + [halo(
            m, b, 7, b.at[1 + q_in, 1, :, pl.ds(1 - k, 2)],
            b.at[3 * k, 1, :, pl.ds(1 - k, 2)], sibling,
        )]

    def corners_out(m, b, c):
        nx = 1 + q_out
        for n, (ny, dy) in enumerate(((0, 1), (2, 0))):
            landed(c[n])
            c.append(halo(
                m, b, 3 + n, b.at[nx, ny, pl.ds(dy, 2), pl.ds(k, 2)],
                b.at[3 - 3 * k, ny, pl.ds(dy, 2), pl.ds(k, 2)], y_peer, has_y, has_y,
            ))

    def corners_in(m, b, c):
        nx = 1 + q_in
        for n, (ny, dy) in enumerate(((0, 1), (2, 0))):
            landed(c[n])
            c.append(halo(
                m, b, 8 + n, b.at[nx, ny, pl.ds(dy, 2), pl.ds(1 - k, 2)],
                b.at[3 * k, ny, pl.ds(dy, 2), pl.ds(1 - k, 2)], sibling,
            ))

    def joined(c):
        for cp in c[2:]:
            landed(cp)

    def cell(a, b, q, cy, cx):
        near = [
            (ny, nx) for ny in STEPS for nx in STEPS
            if abs(cy - ny) <= 1 and abs(cx - nx) <= 1
        ]
        lhs = jnp.concatenate([a(q, ny, nx) for ny, nx in near], axis=1)
        rhs = jnp.concatenate(
            [b[1 + q + nx, 1 + ny, cy - ny + 1, cx - nx + 1] for ny, nx in near], axis=0
        )
        return jnp.dot(lhs, rhs, preferred_element_type=F32)

    spread(0, raw_s, bs)
    c_s_out, c_s_in = side_out(0, bs), side_in(0, bs)
    spread(1, raw_l, bl)
    c_l_out, c_l_in = side_out(1, bl), side_in(1, bl)
    corners_out(0, bs, c_s_out)
    corners_in(0, bs, c_s_in)
    joined(c_s_out)
    joined(c_s_in)
    corners_out(1, bl, c_l_out)

    def left_l(q, ny, nx):
        return bl[1 + q, 1, ny + 1, nx + 1]

    def left_ls(q, ny, nx):
        return ls[q, (ny + 1) * 3 + nx + 1]

    def product(q, left, right, out):
        for d in range(9):
            dy, dx = d // 3, d % 3
            used = jnp.where(q == 0, place[0][d], place[1][d]) < slots
            value = cell(left, right, q, dy - 1, dx - 1)
            out(q, dy, dx, jnp.where(used, value, 0.0).astype(BF16))

    def put_ls(q, dy, dx, value):
        ls[q, dy * 3 + dx] = value

    def put_lsl(q, dy, dx, value):
        bq[1 + q, 1, dy, dx] = value

    product(q_out, left_l, bs, put_ls)
    product(q_in, left_l, bs, put_ls)
    corners_in(1, bl, c_l_in)
    joined(c_l_in)
    product(q_in, left_ls, bl, put_lsl)
    c_q_in = side_in(2, bq)
    joined(c_l_out)
    product(q_out, left_ls, bl, put_lsl)
    c_q_out = side_out(2, bq)
    corners_in(2, bq, c_q_in)
    corners_out(2, bq, c_q_out)
    joined(c_q_in)
    for n, q in enumerate((q_in, q_out)):
        if n == 1:
            joined(c_q_out)
        for d in range(9):
            dy, dx = d // 3, d % 3
            lsl = bq[1 + q, 1, dy, dx].astype(F32)
            kst[q, d] = (3.0 * lsl - 2.0 * cell(left_ls, bq, q, dy - 1, dx - 1)).astype(BF16)
        for b in range(slots):
            kret[q, b] = kst[q, offs[q, b]]
        there = dev(x, y, 4 * h + 2 * k + q, r // 2)
        stay = jnp.logical_and(keeps, at_slot == q)
        cp = send(
            kret.at[q], k_out.at[0, home_row], 0, k_send.at[n], k_recv.at[home_row], there
        )

        @pl.when(jnp.logical_not(stay))
        def _():
            cp.start()

        @pl.when(stay)
        def _():
            pltpu.make_async_copy(kret.at[q], k_out.at[0, home_row], k_recv.at[home_row]).start()

        outs.append((cp, stay))

    for c in (c_s_out, c_s_in, c_l_out, c_l_in, c_q_out, c_q_in):
        for cp in c:
            left(cp)
    for cp, stay in outs:
        @pl.when(jnp.logical_not(stay))
        def _():
            cp.wait_send()
    for j in range(2):
        arrive(k_out.at[0, j], k_recv.at[j])


def on_device(density, intersection, columns, counts):
    size_y = lax.axis_size("gx") // 4
    size_x = lax.axis_size("gy") // 4
    slots = columns.shape[-1]
    block = (128, 128)
    dma = pltpu.SemaphoreType.DMA
    purified = pl.pallas_call(
        functools.partial(kernel, size_x, size_y, slots),
        out_shape=jax.ShapeDtypeStruct(density.shape, BF16),
        in_specs=[
            pl.BlockSpec(memory_space=pl.ANY),
            pl.BlockSpec(memory_space=pl.ANY),
            pl.BlockSpec(memory_space=pl.ANY),
            pl.BlockSpec(memory_space=pl.ANY),
        ],
        out_specs=pl.BlockSpec(memory_space=pl.ANY),
        scratch_shapes=[
            pltpu.SMEM(columns.shape, jnp.int32),
            pltpu.SMEM(counts.shape, jnp.int32),
            dma((2,)),
            pltpu.SMEM((2, slots), jnp.int32),
            pltpu.SMEM((2, slots), jnp.int32),
            pltpu.VMEM((2, slots + 1) + block, BF16),
            pltpu.VMEM((2, slots + 1) + block, BF16),
            pltpu.VMEM((4, 3, 3, 3) + block, BF16),
            pltpu.VMEM((4, 3, 3, 3) + block, BF16),
            pltpu.VMEM((4, 3, 3, 3) + block, BF16),
            pltpu.VMEM((2, 9) + block, BF16),
            pltpu.VMEM((2, 10) + block, BF16),
            pltpu.VMEM((2, slots) + block, BF16),
            dma((2, 2)), dma((2, 2)),
            dma((2,)), dma((2,)),
            dma((3, 10)), dma((3, 10)),
            dma((2,)), dma((2,)),
        ],
        compiler_params=pltpu.CompilerParams(
            collective_id=0, has_side_effects=True, vmem_limit_bytes=60 << 20
        ),
        cost_estimate=pl.CostEstimate(
            flops=3 * 2 * 49 * 2 * 128**3, bytes_accessed=3 << 20, transcendentals=0
        ),
    )(density, intersection, columns, counts)
    return purified.astype(F32)


def solution(mesh):
    placed = (
        P("gx", "gy", None, None, None),
        P("gx", "gy", None, None, None),
        P("gx", "gy", None),
        P("gx", "gy"),
    )
    return jax.shard_map(
        on_device,
        mesh=mesh,
        in_specs=placed,
        out_specs=P("gx", "gy", None, None, None),
        check_vma=False,
    )
```

```python
import functools

import jax
import jax.numpy as jnp
from jax import lax
from jax.experimental import pallas as pl
from jax.experimental.pallas import tpu as pltpu
from jax.sharding import PartitionSpec as P

MESH = pl.DeviceIdType.MESH
BF16 = jnp.bfloat16
F32 = jnp.float32
STEPS = (-1, 0, 1)


def kernel(
    size_x, size_y, slots, l_hbm, s_hbm, cols_hbm, cnts_hbm, k_out,
    cols, cnts, arg_sem, offs_out, offs, raw_s, raw_l, bs, bl, bq, ls, kst, kret,
    t_send, t_recv, o_send, o_recv, h_send, h_recv, k_send, k_recv,
):
    gx = lax.axis_index("gx")
    gy = lax.axis_index("gy")
    y, r = gx // 4, gx % 4
    x, h, k = gy // 4, (gy // 2) % 2, gy % 2
    z = 4 * h + r

    def dev(x_, y_, z_, k_):
        return (y_ * 4 + z_ % 4, (x_ * 2 + z_ // 4) * 2 + k_)

    keeps = r // 2 == k
    at_slot = r % 2
    to = [dev(x, y, 4 * h + 2 * k + j, r // 2) for j in range(2)]
    home = [dev(x, y, 4 * h + 2 * k + q, r // 2) for q in range(2)]
    home_row = r % 2
    stays = [jnp.logical_and(keeps, at_slot == j) for j in range(2)]

    up_z = z + 1
    z_next = dev((x + up_z // 8) % size_x, y, up_z % 8, k)
    dn_z = z + 7
    z_prev = dev((x + size_x - 1 + dn_z // 8) % size_x, y, dn_z % 8, k)
    y_peer = dev(x, (y + size_y - 1 + 2 * k) % size_y, z, 1 - k)
    sibling = dev(x, y, z, 1 - k)
    q_out, q_in = k, 1 - k
    has_next = jnp.logical_or(x < size_x - 1, z < 7)
    has_prev = jnp.logical_or(x > 0, z > 0)
    has_y = jnp.where(k == 0, y > 0, y < size_y - 1)

    pattern_in = [
        pltpu.make_async_copy(cols_hbm, cols, arg_sem.at[0]),
        pltpu.make_async_copy(cnts_hbm, cnts, arg_sem.at[1]),
    ]
    for cp in pattern_in:
        cp.start()
    barrier = pltpu.get_barrier_semaphore()
    pl.semaphore_signal(barrier, inc=1, device_id=sibling, device_id_type=MESH)
    for there, d in ((has_next, z_next), (has_prev, z_prev), (has_y, y_peer)):
        @pl.when(there)
        def _():
            pl.semaphore_signal(barrier, inc=1, device_id=d, device_id_type=MESH)

    for j in range(2):
        @pl.when(jnp.logical_not(stays[j]))
        def _():
            pl.semaphore_signal(barrier, inc=1, device_id=to[j], device_id_type=MESH)
            pl.semaphore_signal(barrier, inc=1, device_id=home[j], device_id_type=MESH)

    for cp in pattern_in:
        cp.wait()
    grid_y = 8 * size_x
    for j in range(2):
        for b in range(slots):
            col = cols[0, j, b]
            dx = col // grid_y - gx
            dy = col % grid_y - (2 * gy + j)
            offs_out[j, b] = jnp.where(b < cnts[0, j], (dy + 1) * 3 + dx + 1, 9)

    zero = jnp.zeros((128, 128), BF16)

    def blank(b, nx, ny):
        def cell_row(i, _):
            b[nx, ny, i // 3, i % 3] = zero
            return 0

        lax.fori_loop(0, 9, cell_row, 0)

    for b in (bs, bl, bq):
        @pl.when(jnp.logical_not(has_prev))
        def _():
            blank(b, 1, 0)
            blank(b, 2, 0)

        @pl.when(jnp.logical_not(has_next))
        def _():
            blank(b, 1, 2)
            blank(b, 2, 2)

        @pl.when(jnp.logical_not(has_y))
        def _():
            for ny in range(3):
                blank(b, 3 * k, ny)

    for q in range(2):
        raw_s[q, slots] = zero
        raw_l[q, slots] = zero
        kst[q, 9] = zero

    pl.semaphore_wait(
        barrier,
        jnp.where(keeps, 3, 5) + jnp.where(has_next, 1, 0) + jnp.where(has_prev, 1, 0)
        + jnp.where(has_y, 1, 0),
    )

    def send(src, dst, j, ssem, rsem, d):
        return pltpu.make_async_remote_copy(
            src_ref=src, dst_ref=dst, send_sem=ssem, recv_sem=rsem,
            device_id=d, device_id_type=MESH,
        )

    def arrive(dst, sem):
        pltpu.make_async_copy(dst, dst, sem).wait()

    live = pl.ds(0, slots)
    outs = []

    def route(src, dst, ssem, rsem, j, d):
        cp = send(src, dst, j, ssem, rsem, d)

        @pl.when(jnp.logical_not(stays[j]))
        def _():
            cp.start()

        @pl.when(stays[j])
        def _():
            pltpu.make_async_copy(src, dst, rsem).start()

        outs.append((cp, stays[j]))

    for j in range(2):
        route(offs_out.at[j], offs.at[at_slot], o_send.at[j], o_recv.at[at_slot], j, to[j])
    def transpose(m, src, raw, when):
        for j in (k, 1 - k):
            stay = jnp.logical_and(keeps, at_slot == j)
            there = dev(x, y, 4 * h + 2 * k + j, r // 2)
            cp = send(
                src.at[0, j], raw.at[at_slot, live], 0,
                t_send.at[m, j], t_recv.at[m, at_slot], there,
            )

            @pl.when(jnp.logical_and(when, jnp.logical_not(stay)))
            def _():
                cp.start()

            @pl.when(jnp.logical_and(when, stay))
            def _():
                pltpu.make_async_copy(
                    src.at[0, j], raw.at[at_slot, live], t_recv.at[m, at_slot]
                ).start()

            if when is light:
                outs.append((cp, stay))

    light = keeps
    heavy = jnp.logical_not(keeps)
    transpose(0, s_hbm, raw_s, heavy)
    transpose(1, l_hbm, raw_l, heavy)
    for q in range(2):
        arrive(offs.at[q], o_recv.at[q])
    transpose(0, s_hbm, raw_s, light)
    transpose(1, l_hbm, raw_l, light)

    place = []
    for q in range(2):
        mine = [offs[q, b] for b in range(slots)]
        row = []
        for d in range(9):
            s = jnp.int32(slots)
            for b in range(slots):
                s = jnp.where(mine[b] == d, b, s)
            row.append(s)
        place.append(row)

    def spread(m, raw, out):
        for q in range(2):
            arrive(raw.at[q, live], t_recv.at[m, q])
        for q in range(2):
            for d in range(9):
                out[1 + q, 1, d // 3, d % 3] = raw[q, place[q][d]]

    def halo(m, b, n, src, dst, d, sent=None, comes=None):
        cp = send(src, dst, 0, h_send.at[m, n], h_recv.at[m, n], d)
        if sent is None:
            cp.start()
        else:
            pl.when(sent)(cp.start)
        return cp, sent, comes

    def landed(c):
        cp, _, comes = c
        if comes is None:
            cp.wait_recv()
        else:
            pl.when(comes)(cp.wait_recv)

    def left(c):
        cp, sent, _ = c
        if sent is None:
            cp.wait_send()
        else:
            pl.when(sent)(cp.wait_send)

    def along_z(m, b, n, q):
        nx = 1 + q
        return [
            halo(
                m, b, n, b.at[nx, 1, pl.ds(1, 2)], b.at[nx, 0, pl.ds(1, 2)],
                z_next, has_next, has_prev,
            ),
            halo(
                m, b, n + 1, b.at[nx, 1, pl.ds(0, 2)], b.at[nx, 2, pl.ds(0, 2)],
                z_prev, has_prev, has_next,
            ),
        ]

    def side_out(m, b):
        return along_z(m, b, 0, q_out) + [halo(
            m, b, 2, b.at[1 + q_out, 1, :, pl.ds(k, 2)],
            b.at[3 - 3 * k, 1, :, pl.ds(k, 2)], y_peer, has_y, has_y,
        )]

    def side_in(m, b):
        return along_z(m, b, 5, q_in) + [halo(
            m, b, 7, b.at[1 + q_in, 1, :, pl.ds(1 - k, 2)],
            b.at[3 * k, 1, :, pl.ds(1 - k, 2)], sibling,
        )]

    def corners_out(m, b, c):
        nx = 1 + q_out
        for n, (ny, dy) in enumerate(((0, 1), (2, 0))):
            landed(c[n])
            c.append(halo(
                m, b, 3 + n, b.at[nx, ny, pl.ds(dy, 2), pl.ds(k, 2)],
                b.at[3 - 3 * k, ny, pl.ds(dy, 2), pl.ds(k, 2)], y_peer, has_y, has_y,
            ))

    def corners_in(m, b, c):
        nx = 1 + q_in
        for n, (ny, dy) in enumerate(((0, 1), (2, 0))):
            landed(c[n])
            c.append(halo(
                m, b, 8 + n, b.at[nx, ny, pl.ds(dy, 2), pl.ds(1 - k, 2)],
                b.at[3 * k, ny, pl.ds(dy, 2), pl.ds(1 - k, 2)], sibling,
            ))

    def joined(c):
        for cp in c[2:]:
            landed(cp)

    def cell(a, b, q, cy, cx):
        near = [
            (ny, nx) for ny in STEPS for nx in STEPS
            if abs(cy - ny) <= 1 and abs(cx - nx) <= 1
        ]
        lhs = jnp.concatenate([a(q, ny, nx) for ny, nx in near], axis=1)
        rhs = jnp.concatenate(
            [b[1 + q + nx, 1 + ny, cy - ny + 1, cx - nx + 1] for ny, nx in near], axis=0
        )
        return jnp.dot(lhs, rhs, preferred_element_type=F32)

    spread(0, raw_s, bs)
    c_s_out, c_s_in = side_out(0, bs), side_in(0, bs)
    spread(1, raw_l, bl)
    c_l_out, c_l_in = side_out(1, bl), side_in(1, bl)
    def left_l(q, ny, nx):
        return bl[1 + q, 1, ny + 1, nx + 1]

    def left_ls(q, ny, nx):
        return ls[q, (ny + 1) * 3 + nx + 1]

    def product(q, left, right, out):
        for d in range(9):
            dy, dx = d // 3, d % 3
            used = jnp.where(q == 0, place[0][d], place[1][d]) < slots
            value = cell(left, right, q, dy - 1, dx - 1)
            out(q, dy, dx, jnp.where(used, value, 0.0).astype(BF16))

    def put_ls(q, dy, dx, value):
        ls[q, dy * 3 + dx] = value

    def put_lsl(q, dy, dx, value):
        bq[1 + q, 1, dy, dx] = value

    corners_out(0, bs, c_s_out)
    corners_in(0, bs, c_s_in)
    joined(c_s_in)
    product(q_in, left_l, bs, put_ls)
    corners_in(1, bl, c_l_in)
    corners_out(1, bl, c_l_out)
    joined(c_l_in)
    product(q_in, left_ls, bl, put_lsl)
    c_q_in = side_in(2, bq)
    joined(c_s_out)
    product(q_out, left_l, bs, put_ls)
    joined(c_l_out)
    product(q_out, left_ls, bl, put_lsl)
    c_q_out = side_out(2, bq)
    corners_in(2, bq, c_q_in)
    corners_out(2, bq, c_q_out)
    joined(c_q_in)
    for n, q in enumerate((q_in, q_out)):
        if n == 1:
            joined(c_q_out)
        for d in range(9):
            dy, dx = d // 3, d % 3
            lsl = bq[1 + q, 1, dy, dx].astype(F32)
            kst[q, d] = (3.0 * lsl - 2.0 * cell(left_ls, bq, q, dy - 1, dx - 1)).astype(BF16)
        for b in range(slots):
            kret[q, b] = kst[q, offs[q, b]]
        there = dev(x, y, 4 * h + 2 * k + q, r // 2)
        stay = jnp.logical_and(keeps, at_slot == q)
        cp = send(
            kret.at[q], k_out.at[0, home_row], 0, k_send.at[n], k_recv.at[home_row], there
        )

        @pl.when(jnp.logical_not(stay))
        def _():
            cp.start()

        @pl.when(stay)
        def _():
            pltpu.make_async_copy(kret.at[q], k_out.at[0, home_row], k_recv.at[home_row]).start()

        outs.append((cp, stay))

    for c in (c_s_out, c_s_in, c_l_out, c_l_in, c_q_out, c_q_in):
        for cp in c:
            left(cp)
    for cp, stay in outs:
        @pl.when(jnp.logical_not(stay))
        def _():
            cp.wait_send()
    for j in range(2):
        arrive(k_out.at[0, j], k_recv.at[j])


def on_device(density, intersection, columns, counts):
    size_y = lax.axis_size("gx") // 4
    size_x = lax.axis_size("gy") // 4
    slots = columns.shape[-1]
    block = (128, 128)
    dma = pltpu.SemaphoreType.DMA
    purified = pl.pallas_call(
        functools.partial(kernel, size_x, size_y, slots),
        out_shape=jax.ShapeDtypeStruct(density.shape, BF16),
        in_specs=[
            pl.BlockSpec(memory_space=pl.ANY),
            pl.BlockSpec(memory_space=pl.ANY),
            pl.BlockSpec(memory_space=pl.ANY),
            pl.BlockSpec(memory_space=pl.ANY),
        ],
        out_specs=pl.BlockSpec(memory_space=pl.ANY),
        scratch_shapes=[
            pltpu.SMEM(columns.shape, jnp.int32),
            pltpu.SMEM(counts.shape, jnp.int32),
            dma((2,)),
            pltpu.SMEM((2, slots), jnp.int32),
            pltpu.SMEM((2, slots), jnp.int32),
            pltpu.VMEM((2, slots + 1) + block, BF16),
            pltpu.VMEM((2, slots + 1) + block, BF16),
            pltpu.VMEM((4, 3, 3, 3) + block, BF16),
            pltpu.VMEM((4, 3, 3, 3) + block, BF16),
            pltpu.VMEM((4, 3, 3, 3) + block, BF16),
            pltpu.VMEM((2, 9) + block, BF16),
            pltpu.VMEM((2, 10) + block, BF16),
            pltpu.VMEM((2, slots) + block, BF16),
            dma((2, 2)), dma((2, 2)),
            dma((2,)), dma((2,)),
            dma((3, 10)), dma((3, 10)),
            dma((2,)), dma((2,)),
        ],
        compiler_params=pltpu.CompilerParams(
            collective_id=0, has_side_effects=True, vmem_limit_bytes=60 << 20
        ),
        cost_estimate=pl.CostEstimate(
            flops=3 * 2 * 49 * 2 * 128**3, bytes_accessed=3 << 20, transcendentals=0
        ),
    )(density, intersection, columns, counts)
    return purified.astype(F32)


def solution(mesh):
    placed = (
        P("gx", "gy", None, None, None),
        P("gx", "gy", None, None, None),
        P("gx", "gy", None),
        P("gx", "gy"),
    )
    return jax.shard_map(
        on_device,
        mesh=mesh,
        in_specs=placed,
        out_specs=P("gx", "gy", None, None, None),
        check_vma=False,
    )
```

```python
import functools

import jax
import jax.numpy as jnp
from jax import lax
from jax.experimental import pallas as pl
from jax.experimental.pallas import tpu as pltpu
from jax.sharding import PartitionSpec as P

MESH = pl.DeviceIdType.MESH
BF16 = jnp.bfloat16
F32 = jnp.float32
STEPS = (-1, 0, 1)


def kernel(
    size_x, size_y, slots, l_hbm, s_hbm, cols_hbm, cnts_hbm, k_out,
    cols, cnts, arg_sem, offs_out, offs, raw_s, raw_l, bs, bl, bq, ls, kst, kret,
    t_send, t_recv, o_send, o_recv, h_send, h_recv, k_send, k_recv,
):
    gx = lax.axis_index("gx")
    gy = lax.axis_index("gy")
    y, r = gx // 4, gx % 4
    x, h, k = gy // 4, (gy // 2) % 2, gy % 2
    z = 4 * h + r

    def dev(x_, y_, z_, k_):
        return (y_ * 4 + z_ % 4, (x_ * 2 + z_ // 4) * 2 + k_)

    keeps = r // 2 == k
    at_slot = r % 2
    to = [dev(x, y, 4 * h + 2 * k + j, r // 2) for j in range(2)]
    home = [dev(x, y, 4 * h + 2 * k + q, r // 2) for q in range(2)]
    home_row = r % 2
    stays = [jnp.logical_and(keeps, at_slot == j) for j in range(2)]

    up_z = z + 1
    z_next = dev((x + up_z // 8) % size_x, y, up_z % 8, k)
    dn_z = z + 7
    z_prev = dev((x + size_x - 1 + dn_z // 8) % size_x, y, dn_z % 8, k)
    y_peer = dev(x, (y + size_y - 1 + 2 * k) % size_y, z, 1 - k)
    sibling = dev(x, y, z, 1 - k)
    q_out, q_in = k, 1 - k
    has_next = jnp.logical_or(x < size_x - 1, z < 7)
    has_prev = jnp.logical_or(x > 0, z > 0)
    has_y = jnp.where(k == 0, y > 0, y < size_y - 1)

    pattern_in = [
        pltpu.make_async_copy(cols_hbm, cols, arg_sem.at[0]),
        pltpu.make_async_copy(cnts_hbm, cnts, arg_sem.at[1]),
    ]
    for cp in pattern_in:
        cp.start()
    barrier = pltpu.get_barrier_semaphore()
    pl.semaphore_signal(barrier, inc=1, device_id=sibling, device_id_type=MESH)
    for there, d in ((has_next, z_next), (has_prev, z_prev), (has_y, y_peer)):
        @pl.when(there)
        def _():
            pl.semaphore_signal(barrier, inc=1, device_id=d, device_id_type=MESH)

    for j in range(2):
        @pl.when(jnp.logical_not(stays[j]))
        def _():
            pl.semaphore_signal(barrier, inc=1, device_id=to[j], device_id_type=MESH)
            pl.semaphore_signal(barrier, inc=1, device_id=home[j], device_id_type=MESH)

    for cp in pattern_in:
        cp.wait()
    grid_y = 8 * size_x
    for j in range(2):
        for b in range(slots):
            col = cols[0, j, b]
            dx = col // grid_y - gx
            dy = col % grid_y - (2 * gy + j)
            offs_out[j, b] = jnp.where(b < cnts[0, j], (dy + 1) * 3 + dx + 1, 9)

    zero = jnp.zeros((128, 128), BF16)

    def blank(b, nx, ny):
        def cell_row(i, _):
            b[nx, ny, i // 3, i % 3] = zero
            return 0

        lax.fori_loop(0, 9, cell_row, 0)

    for b in (bs, bl, bq):
        @pl.when(jnp.logical_not(has_prev))
        def _():
            blank(b, 1, 0)
            blank(b, 2, 0)

        @pl.when(jnp.logical_not(has_next))
        def _():
            blank(b, 1, 2)
            blank(b, 2, 2)

        @pl.when(jnp.logical_not(has_y))
        def _():
            for ny in range(3):
                blank(b, 3 * k, ny)

    for q in range(2):
        raw_s[q, slots] = zero
        raw_l[q, slots] = zero
        kst[q, 9] = zero

    pl.semaphore_wait(
        barrier,
        jnp.where(keeps, 3, 5) + jnp.where(has_next, 1, 0) + jnp.where(has_prev, 1, 0)
        + jnp.where(has_y, 1, 0),
    )

    def send(src, dst, j, ssem, rsem, d):
        return pltpu.make_async_remote_copy(
            src_ref=src, dst_ref=dst, send_sem=ssem, recv_sem=rsem,
            device_id=d, device_id_type=MESH,
        )

    def arrive(dst, sem):
        pltpu.make_async_copy(dst, dst, sem).wait()

    live = pl.ds(0, slots)
    outs = []

    def route(src, dst, ssem, rsem, j, d):
        cp = send(src, dst, j, ssem, rsem, d)

        @pl.when(jnp.logical_not(stays[j]))
        def _():
            cp.start()

        @pl.when(stays[j])
        def _():
            pltpu.make_async_copy(src, dst, rsem).start()

        outs.append((cp, stays[j]))

    for j in range(2):
        route(offs_out.at[j], offs.at[at_slot], o_send.at[j], o_recv.at[at_slot], j, to[j])
    def transpose(m, src, raw, when):
        for j in (k, 1 - k):
            stay = jnp.logical_and(keeps, at_slot == j)
            there = dev(x, y, 4 * h + 2 * k + j, r // 2)
            cp = send(
                src.at[0, j], raw.at[at_slot, live], 0,
                t_send.at[m, j], t_recv.at[m, at_slot], there,
            )

            @pl.when(jnp.logical_and(when, jnp.logical_not(stay)))
            def _():
                cp.start()

            @pl.when(jnp.logical_and(when, stay))
            def _():
                pltpu.make_async_copy(
                    src.at[0, j], raw.at[at_slot, live], t_recv.at[m, at_slot]
                ).start()

            if when is light:
                outs.append((cp, stay))

    light = keeps
    heavy = jnp.logical_not(keeps)
    transpose(0, s_hbm, raw_s, heavy)
    transpose(1, l_hbm, raw_l, heavy)
    for q in range(2):
        arrive(offs.at[q], o_recv.at[q])
    transpose(0, s_hbm, raw_s, light)
    transpose(1, l_hbm, raw_l, light)

    place = []
    for q in range(2):
        mine = [offs[q, b] for b in range(slots)]
        row = []
        for d in range(9):
            s = jnp.int32(slots)
            for b in range(slots):
                s = jnp.where(mine[b] == d, b, s)
            row.append(s)
        place.append(row)

    def spread(m, raw, out):
        for q in range(2):
            arrive(raw.at[q, live], t_recv.at[m, q])
        for q in range(2):
            for d in range(9):
                out[1 + q, 1, d // 3, d % 3] = raw[q, place[q][d]]

    def halo(m, b, n, src, dst, d, sent=None, comes=None):
        cp = send(src, dst, 0, h_send.at[m, n], h_recv.at[m, n], d)
        if sent is None:
            cp.start()
        else:
            pl.when(sent)(cp.start)
        return cp, sent, comes

    def landed(c):
        cp, _, comes = c
        if comes is None:
            cp.wait_recv()
        else:
            pl.when(comes)(cp.wait_recv)

    def left(c):
        cp, sent, _ = c
        if sent is None:
            cp.wait_send()
        else:
            pl.when(sent)(cp.wait_send)

    def along_z(m, b, n, q):
        nx = 1 + q
        return [
            halo(
                m, b, n, b.at[nx, 1, pl.ds(1, 2)], b.at[nx, 0, pl.ds(1, 2)],
                z_next, has_next, has_prev,
            ),
            halo(
                m, b, n + 1, b.at[nx, 1, pl.ds(0, 2)], b.at[nx, 2, pl.ds(0, 2)],
                z_prev, has_prev, has_next,
            ),
        ]

    def side_out(m, b):
        return along_z(m, b, 0, q_out) + [halo(
            m, b, 2, b.at[1 + q_out, 1, :, pl.ds(k, 2)],
            b.at[3 - 3 * k, 1, :, pl.ds(k, 2)], y_peer, has_y, has_y,
        )]

    def side_in(m, b):
        return along_z(m, b, 5, q_in) + [halo(
            m, b, 7, b.at[1 + q_in, 1, :, pl.ds(1 - k, 2)],
            b.at[3 * k, 1, :, pl.ds(1 - k, 2)], sibling,
        )]

    def corners_out(m, b, c):
        nx = 1 + q_out
        for n, (ny, dy) in enumerate(((0, 1), (2, 0))):
            landed(c[n])
            c.append(halo(
                m, b, 3 + n, b.at[nx, ny, pl.ds(dy, 2), pl.ds(k, 2)],
                b.at[3 - 3 * k, ny, pl.ds(dy, 2), pl.ds(k, 2)], y_peer, has_y, has_y,
            ))

    def corners_in(m, b, c):
        nx = 1 + q_in
        for n, (ny, dy) in enumerate(((0, 1), (2, 0))):
            landed(c[n])
            c.append(halo(
                m, b, 8 + n, b.at[nx, ny, pl.ds(dy, 2), pl.ds(1 - k, 2)],
                b.at[3 * k, ny, pl.ds(dy, 2), pl.ds(1 - k, 2)], sibling,
            ))

    def joined(c):
        for cp in c[2:]:
            landed(cp)

    def cell(a, b, q, cy, cx):
        near = [
            (ny, nx) for ny in STEPS for nx in STEPS
            if abs(cy - ny) <= 1 and abs(cx - nx) <= 1
        ]
        lhs = jnp.concatenate([a(q, ny, nx) for ny, nx in near], axis=1)
        rhs = jnp.concatenate(
            [b[1 + q + nx, 1 + ny, cy - ny + 1, cx - nx + 1] for ny, nx in near], axis=0
        )
        return jnp.dot(lhs, rhs, preferred_element_type=F32)

    spread(0, raw_s, bs)
    c_s_out, c_s_in = side_out(0, bs), side_in(0, bs)
    spread(1, raw_l, bl)
    c_l_in, c_l_out = side_in(1, bl), side_out(1, bl)
    def left_l(q, ny, nx):
        return bl[1 + q, 1, ny + 1, nx + 1]

    def left_ls(q, ny, nx):
        return ls[q, (ny + 1) * 3 + nx + 1]

    def cells(a, b, q, cy):
        near = [(ny, nx) for ny in STEPS for nx in STEPS if abs(cy - ny) <= 1]
        lhs = jnp.concatenate([a(q, ny, nx) for ny, nx in near], axis=1)
        rhs = jnp.concatenate([
            jnp.concatenate([
                b[1 + q + nx, 1 + ny, cy - ny + 1, cx - nx + 1] if cx - nx >= -1 else zero
                for cx in (-1, 0)
            ], axis=1)
            for ny, nx in near
        ], axis=0)
        both = jnp.dot(lhs, rhs, preferred_element_type=F32)
        return both[:, :128], both[:, 128:], cell(a, b, q, cy, 1)

    def product(q, left, right, out):
        for d in range(9):
            dy, dx = d // 3, d % 3
            if dx == 0:
                three = cells(left, right, q, dy - 1)
            used = jnp.where(q == 0, place[0][d], place[1][d]) < slots
            value = three[dx]
            out(q, dy, dx, jnp.where(used, value, 0.0).astype(BF16))

    def put_ls(q, dy, dx, value):
        ls[q, dy * 3 + dx] = value

    def put_lsl(q, dy, dx, value):
        bq[1 + q, 1, dy, dx] = value

    corners_out(0, bs, c_s_out)
    corners_in(0, bs, c_s_in)
    joined(c_s_in)
    product(q_in, left_l, bs, put_ls)
    corners_in(1, bl, c_l_in)
    corners_out(1, bl, c_l_out)
    joined(c_l_in)
    product(q_in, left_ls, bl, put_lsl)
    c_q_in = side_in(2, bq)
    joined(c_s_out)
    product(q_out, left_l, bs, put_ls)
    joined(c_l_out)
    product(q_out, left_ls, bl, put_lsl)
    c_q_out = side_out(2, bq)
    corners_in(2, bq, c_q_in)
    corners_out(2, bq, c_q_out)
    joined(c_q_in)
    for n, q in enumerate((q_in, q_out)):
        if n == 1:
            joined(c_q_out)
        for d in range(9):
            dy, dx = d // 3, d % 3
            if dx == 0:
                three = cells(left_ls, bq, q, dy - 1)
            lsl = bq[1 + q, 1, dy, dx].astype(F32)
            kst[q, d] = (3.0 * lsl - 2.0 * three[dx]).astype(BF16)
        for b in range(slots):
            kret[q, b] = kst[q, offs[q, b]]
        there = dev(x, y, 4 * h + 2 * k + q, r // 2)
        stay = jnp.logical_and(keeps, at_slot == q)
        cp = send(
            kret.at[q], k_out.at[0, home_row], 0, k_send.at[n], k_recv.at[home_row], there
        )

        @pl.when(jnp.logical_not(stay))
        def _():
            cp.start()

        @pl.when(stay)
        def _():
            pltpu.make_async_copy(kret.at[q], k_out.at[0, home_row], k_recv.at[home_row]).start()

        outs.append((cp, stay))

    for c in (c_s_out, c_s_in, c_l_out, c_l_in, c_q_out, c_q_in):
        for cp in c:
            left(cp)
    for cp, stay in outs:
        @pl.when(jnp.logical_not(stay))
        def _():
            cp.wait_send()
    for j in range(2):
        arrive(k_out.at[0, j], k_recv.at[j])


def on_device(density, intersection, columns, counts):
    size_y = lax.axis_size("gx") // 4
    size_x = lax.axis_size("gy") // 4
    slots = columns.shape[-1]
    block = (128, 128)
    dma = pltpu.SemaphoreType.DMA
    purified = pl.pallas_call(
        functools.partial(kernel, size_x, size_y, slots),
        out_shape=jax.ShapeDtypeStruct(density.shape, BF16),
        in_specs=[
            pl.BlockSpec(memory_space=pl.ANY),
            pl.BlockSpec(memory_space=pl.ANY),
            pl.BlockSpec(memory_space=pl.ANY),
            pl.BlockSpec(memory_space=pl.ANY),
        ],
        out_specs=pl.BlockSpec(memory_space=pl.ANY),
        scratch_shapes=[
            pltpu.SMEM(columns.shape, jnp.int32),
            pltpu.SMEM(counts.shape, jnp.int32),
            dma((2,)),
            pltpu.SMEM((2, slots), jnp.int32),
            pltpu.SMEM((2, slots), jnp.int32),
            pltpu.VMEM((2, slots + 1) + block, BF16),
            pltpu.VMEM((2, slots + 1) + block, BF16),
            pltpu.VMEM((4, 3, 3, 3) + block, BF16),
            pltpu.VMEM((4, 3, 3, 3) + block, BF16),
            pltpu.VMEM((4, 3, 3, 3) + block, BF16),
            pltpu.VMEM((2, 9) + block, BF16),
            pltpu.VMEM((2, 10) + block, BF16),
            pltpu.VMEM((2, slots) + block, BF16),
            dma((2, 2)), dma((2, 2)),
            dma((2,)), dma((2,)),
            dma((3, 10)), dma((3, 10)),
            dma((2,)), dma((2,)),
        ],
        compiler_params=pltpu.CompilerParams(
            collective_id=0, has_side_effects=True, vmem_limit_bytes=60 << 20
        ),
        cost_estimate=pl.CostEstimate(
            flops=3 * 2 * 49 * 2 * 128**3, bytes_accessed=3 << 20, transcendentals=0
        ),
    )(density, intersection, columns, counts)
    return purified.astype(F32)


def solution(mesh):
    placed = (
        P("gx", "gy", None, None, None),
        P("gx", "gy", None, None, None),
        P("gx", "gy", None),
        P("gx", "gy"),
    )
    return jax.shard_map(
        on_device,
        mesh=mesh,
        in_specs=placed,
        out_specs=P("gx", "gy", None, None, None),
        check_vma=False,
    )
```

```python
import functools

import jax
import jax.numpy as jnp
from jax import lax
from jax.experimental import pallas as pl
from jax.experimental.pallas import tpu as pltpu
from jax.sharding import PartitionSpec as P

MESH = pl.DeviceIdType.MESH
BF16 = jnp.bfloat16
F32 = jnp.float32
STEPS = (-1, 0, 1)


def kernel(
    size_x, size_y, slots, l_hbm, s_hbm, cols_hbm, cnts_hbm, k_out,
    cols, cnts, arg_sem, offs_out, offs, raw_s, raw_l, bs, bl, bq, ls, kst, kret,
    t_send, t_recv, o_send, o_recv, h_send, h_recv, k_send, k_recv,
):
    gx = lax.axis_index("gx")
    gy = lax.axis_index("gy")
    y, r = gx // 4, gx % 4
    x, h, k = gy // 4, (gy // 2) % 2, gy % 2
    z = 4 * h + r

    def dev(x_, y_, z_, k_):
        return (y_ * 4 + z_ % 4, (x_ * 2 + z_ // 4) * 2 + k_)

    keeps = r // 2 == k
    at_slot = r % 2
    to = [dev(x, y, 4 * h + 2 * k + j, r // 2) for j in range(2)]
    home = [dev(x, y, 4 * h + 2 * k + q, r // 2) for q in range(2)]
    home_row = r % 2
    stays = [jnp.logical_and(keeps, at_slot == j) for j in range(2)]

    up_z = z + 1
    z_next = dev((x + up_z // 8) % size_x, y, up_z % 8, k)
    dn_z = z + 7
    z_prev = dev((x + size_x - 1 + dn_z // 8) % size_x, y, dn_z % 8, k)
    y_peer = dev(x, (y + size_y - 1 + 2 * k) % size_y, z, 1 - k)
    sibling = dev(x, y, z, 1 - k)
    q_out, q_in = k, 1 - k
    has_next = jnp.logical_or(x < size_x - 1, z < 7)
    has_prev = jnp.logical_or(x > 0, z > 0)
    has_y = jnp.where(k == 0, y > 0, y < size_y - 1)

    pattern_in = [
        pltpu.make_async_copy(cols_hbm, cols, arg_sem.at[0]),
        pltpu.make_async_copy(cnts_hbm, cnts, arg_sem.at[1]),
    ]
    for cp in pattern_in:
        cp.start()
    barrier = pltpu.get_barrier_semaphore()
    pl.semaphore_signal(barrier, inc=1, device_id=sibling, device_id_type=MESH)
    for there, d in ((has_next, z_next), (has_prev, z_prev), (has_y, y_peer)):
        @pl.when(there)
        def _():
            pl.semaphore_signal(barrier, inc=1, device_id=d, device_id_type=MESH)

    for j in range(2):
        @pl.when(jnp.logical_not(stays[j]))
        def _():
            pl.semaphore_signal(barrier, inc=1, device_id=to[j], device_id_type=MESH)
            pl.semaphore_signal(barrier, inc=1, device_id=home[j], device_id_type=MESH)

    for cp in pattern_in:
        cp.wait()
    grid_y = 8 * size_x
    for j in range(2):
        for b in range(slots):
            col = cols[0, j, b]
            dx = col // grid_y - gx
            dy = col % grid_y - (2 * gy + j)
            offs_out[j, b] = jnp.where(b < cnts[0, j], (dy + 1) * 3 + dx + 1, 9)

    zero = jnp.zeros((128, 128), BF16)

    def blank(b, nx, ny):
        def cell_row(i, _):
            b[nx, ny, i // 3, i % 3] = zero
            return 0

        lax.fori_loop(0, 9, cell_row, 0)

    for b in (bs, bl, bq):
        @pl.when(jnp.logical_not(has_prev))
        def _():
            blank(b, 1, 0)
            blank(b, 2, 0)

        @pl.when(jnp.logical_not(has_next))
        def _():
            blank(b, 1, 2)
            blank(b, 2, 2)

        @pl.when(jnp.logical_not(has_y))
        def _():
            for ny in range(3):
                blank(b, 3 * k, ny)

    for q in range(2):
        raw_s[q, slots] = zero
        raw_l[q, slots] = zero
        kst[q, 9] = zero

    pl.semaphore_wait(
        barrier,
        jnp.where(keeps, 3, 5) + jnp.where(has_next, 1, 0) + jnp.where(has_prev, 1, 0)
        + jnp.where(has_y, 1, 0),
    )

    def send(src, dst, j, ssem, rsem, d):
        return pltpu.make_async_remote_copy(
            src_ref=src, dst_ref=dst, send_sem=ssem, recv_sem=rsem,
            device_id=d, device_id_type=MESH,
        )

    def arrive(dst, sem):
        pltpu.make_async_copy(dst, dst, sem).wait()

    live = pl.ds(0, slots)
    outs = []

    def route(src, dst, ssem, rsem, j, d):
        cp = send(src, dst, j, ssem, rsem, d)

        @pl.when(jnp.logical_not(stays[j]))
        def _():
            cp.start()

        @pl.when(stays[j])
        def _():
            pltpu.make_async_copy(src, dst, rsem).start()

        outs.append((cp, stays[j]))

    for j in range(2):
        route(offs_out.at[j], offs.at[at_slot], o_send.at[j], o_recv.at[at_slot], j, to[j])
    def transpose(m, src, raw, when):
        for j in (k, 1 - k):
            stay = jnp.logical_and(keeps, at_slot == j)
            there = dev(x, y, 4 * h + 2 * k + j, r // 2)
            cp = send(
                src.at[0, j], raw.at[at_slot, live], 0,
                t_send.at[m, j], t_recv.at[m, at_slot], there,
            )

            @pl.when(jnp.logical_and(when, jnp.logical_not(stay)))
            def _():
                cp.start()

            @pl.when(jnp.logical_and(when, stay))
            def _():
                pltpu.make_async_copy(
                    src.at[0, j], raw.at[at_slot, live], t_recv.at[m, at_slot]
                ).start()

            if when is light:
                outs.append((cp, stay))

    light = keeps
    heavy = jnp.logical_not(keeps)
    transpose(0, s_hbm, raw_s, heavy)
    transpose(1, l_hbm, raw_l, heavy)
    for q in range(2):
        arrive(offs.at[q], o_recv.at[q])
    transpose(0, s_hbm, raw_s, light)
    transpose(1, l_hbm, raw_l, light)

    place = []
    for q in range(2):
        mine = [offs[q, b] for b in range(slots)]
        row = []
        for d in range(9):
            s = jnp.int32(slots)
            for b in range(slots):
                s = jnp.where(mine[b] == d, b, s)
            row.append(s)
        place.append(row)

    def spread(m, raw, out):
        for q in range(2):
            arrive(raw.at[q, live], t_recv.at[m, q])
        for q in range(2):
            for d in range(9):
                out[1 + q, 1, d // 3, d % 3] = raw[q, place[q][d]]

    def halo(m, b, n, src, dst, d, sent=None, comes=None):
        cp = send(src, dst, 0, h_send.at[m, n], h_recv.at[m, n], d)
        if sent is None:
            cp.start()
        else:
            pl.when(sent)(cp.start)
        return cp, sent, comes

    def landed(c):
        cp, _, comes = c
        if comes is None:
            cp.wait_recv()
        else:
            pl.when(comes)(cp.wait_recv)

    def left(c):
        cp, sent, _ = c
        if sent is None:
            cp.wait_send()
        else:
            pl.when(sent)(cp.wait_send)

    def along_z(m, b, n, q):
        nx = 1 + q
        return [
            halo(
                m, b, n, b.at[nx, 1, pl.ds(1, 2)], b.at[nx, 0, pl.ds(1, 2)],
                z_next, has_next, has_prev,
            ),
            halo(
                m, b, n + 1, b.at[nx, 1, pl.ds(0, 2)], b.at[nx, 2, pl.ds(0, 2)],
                z_prev, has_prev, has_next,
            ),
        ]

    def side_out(m, b):
        return along_z(m, b, 0, q_out) + [halo(
            m, b, 2, b.at[1 + q_out, 1, :, pl.ds(k, 2)],
            b.at[3 - 3 * k, 1, :, pl.ds(k, 2)], y_peer, has_y, has_y,
        )]

    def side_in(m, b):
        return along_z(m, b, 5, q_in) + [halo(
            m, b, 7, b.at[1 + q_in, 1, :, pl.ds(1 - k, 2)],
            b.at[3 * k, 1, :, pl.ds(1 - k, 2)], sibling,
        )]

    def corners_out(m, b, c):
        nx = 1 + q_out
        for n, (ny, dy) in enumerate(((0, 1), (2, 0))):
            landed(c[n])
            c.append(halo(
                m, b, 3 + n, b.at[nx, ny, pl.ds(dy, 2), pl.ds(k, 2)],
                b.at[3 - 3 * k, ny, pl.ds(dy, 2), pl.ds(k, 2)], y_peer, has_y, has_y,
            ))

    def corners_in(m, b, c):
        nx = 1 + q_in
        for n, (ny, dy) in enumerate(((0, 1), (2, 0))):
            landed(c[n])
            c.append(halo(
                m, b, 8 + n, b.at[nx, ny, pl.ds(dy, 2), pl.ds(1 - k, 2)],
                b.at[3 * k, ny, pl.ds(dy, 2), pl.ds(1 - k, 2)], sibling,
            ))

    def joined(c):
        for cp in c[2:]:
            landed(cp)

    def cell(a, b, q, cy, cx):
        near = [
            (ny, nx) for ny in STEPS for nx in STEPS
            if abs(cy - ny) <= 1 and abs(cx - nx) <= 1
        ]
        lhs = jnp.concatenate([a(q, ny, nx) for ny, nx in near], axis=1)
        rhs = jnp.concatenate(
            [b[1 + q + nx, 1 + ny, cy - ny + 1, cx - nx + 1] for ny, nx in near], axis=0
        )
        return jnp.dot(lhs, rhs, preferred_element_type=F32)

    spread(0, raw_s, bs)
    c_s_in, c_s_out = side_in(0, bs), side_out(0, bs)
    spread(1, raw_l, bl)
    c_l_in, c_l_out = side_in(1, bl), side_out(1, bl)
    def left_l(q, ny, nx):
        return bl[1 + q, 1, ny + 1, nx + 1]

    def left_ls(q, ny, nx):
        return ls[q, (ny + 1) * 3 + nx + 1]

    def cells(a, b, q, cy):
        near = [(ny, nx) for ny in STEPS for nx in STEPS if abs(cy - ny) <= 1]
        lhs = jnp.concatenate([a(q, ny, nx) for ny, nx in near], axis=1)
        rhs = jnp.concatenate([
            jnp.concatenate([
                b[1 + q + nx, 1 + ny, cy - ny + 1, cx - nx + 1] if cx - nx >= -1 else zero
                for cx in (-1, 0)
            ], axis=1)
            for ny, nx in near
        ], axis=0)
        both = jnp.dot(lhs, rhs, preferred_element_type=F32)
        return both[:, :128], both[:, 128:], cell(a, b, q, cy, 1)

    def product(q, left, right, out):
        for d in range(9):
            dy, dx = d // 3, d % 3
            if dx == 0:
                three = cells(left, right, q, dy - 1)
            used = jnp.where(q == 0, place[0][d], place[1][d]) < slots
            value = three[dx]
            out(q, dy, dx, jnp.where(used, value, 0.0).astype(BF16))

    def put_ls(q, dy, dx, value):
        ls[q, dy * 3 + dx] = value

    def put_lsl(q, dy, dx, value):
        bq[1 + q, 1, dy, dx] = value

    corners_in(0, bs, c_s_in)
    corners_out(0, bs, c_s_out)
    joined(c_s_in)
    product(q_in, left_l, bs, put_ls)
    corners_in(1, bl, c_l_in)
    corners_out(1, bl, c_l_out)
    joined(c_l_in)
    product(q_in, left_ls, bl, put_lsl)
    c_q_in = side_in(2, bq)
    joined(c_s_out)
    product(q_out, left_l, bs, put_ls)
    joined(c_l_out)
    product(q_out, left_ls, bl, put_lsl)
    c_q_out = side_out(2, bq)
    corners_in(2, bq, c_q_in)
    corners_out(2, bq, c_q_out)
    joined(c_q_in)
    for n, q in enumerate((q_in, q_out)):
        if n == 1:
            joined(c_q_out)
        for d in range(9):
            dy, dx = d // 3, d % 3
            if dx == 0:
                three = cells(left_ls, bq, q, dy - 1)
            lsl = bq[1 + q, 1, dy, dx].astype(F32)
            kst[q, d] = (3.0 * lsl - 2.0 * three[dx]).astype(BF16)
        for b in range(slots):
            kret[q, b] = kst[q, offs[q, b]]
        there = dev(x, y, 4 * h + 2 * k + q, r // 2)
        stay = jnp.logical_and(keeps, at_slot == q)
        cp = send(
            kret.at[q], k_out.at[0, home_row], 0, k_send.at[n], k_recv.at[home_row], there
        )

        @pl.when(jnp.logical_not(stay))
        def _():
            cp.start()

        @pl.when(stay)
        def _():
            pltpu.make_async_copy(kret.at[q], k_out.at[0, home_row], k_recv.at[home_row]).start()

        outs.append((cp, stay))

    for c in (c_s_out, c_s_in, c_l_out, c_l_in, c_q_out, c_q_in):
        for cp in c:
            left(cp)
    for cp, stay in outs:
        @pl.when(jnp.logical_not(stay))
        def _():
            cp.wait_send()
    for j in range(2):
        arrive(k_out.at[0, j], k_recv.at[j])


def on_device(density, intersection, columns, counts):
    size_y = lax.axis_size("gx") // 4
    size_x = lax.axis_size("gy") // 4
    slots = columns.shape[-1]
    block = (128, 128)
    dma = pltpu.SemaphoreType.DMA
    purified = pl.pallas_call(
        functools.partial(kernel, size_x, size_y, slots),
        out_shape=jax.ShapeDtypeStruct(density.shape, BF16),
        in_specs=[
            pl.BlockSpec(memory_space=pl.ANY),
            pl.BlockSpec(memory_space=pl.ANY),
            pl.BlockSpec(memory_space=pl.ANY),
            pl.BlockSpec(memory_space=pl.ANY),
        ],
        out_specs=pl.BlockSpec(memory_space=pl.ANY),
        scratch_shapes=[
            pltpu.SMEM(columns.shape, jnp.int32),
            pltpu.SMEM(counts.shape, jnp.int32),
            dma((2,)),
            pltpu.SMEM((2, slots), jnp.int32),
            pltpu.SMEM((2, slots), jnp.int32),
            pltpu.VMEM((2, slots + 1) + block, BF16),
            pltpu.VMEM((2, slots + 1) + block, BF16),
            pltpu.VMEM((4, 3, 3, 3) + block, BF16),
            pltpu.VMEM((4, 3, 3, 3) + block, BF16),
            pltpu.VMEM((4, 3, 3, 3) + block, BF16),
            pltpu.VMEM((2, 9) + block, BF16),
            pltpu.VMEM((2, 10) + block, BF16),
            pltpu.VMEM((2, slots) + block, BF16),
            dma((2, 2)), dma((2, 2)),
            dma((2,)), dma((2,)),
            dma((3, 10)), dma((3, 10)),
            dma((2,)), dma((2,)),
        ],
        compiler_params=pltpu.CompilerParams(
            collective_id=0, has_side_effects=True, vmem_limit_bytes=60 << 20
        ),
        cost_estimate=pl.CostEstimate(
            flops=3 * 2 * 49 * 2 * 128**3, bytes_accessed=3 << 20, transcendentals=0
        ),
    )(density, intersection, columns, counts)
    return purified.astype(F32)


def solution(mesh):
    placed = (
        P("gx", "gy", None, None, None),
        P("gx", "gy", None, None, None),
        P("gx", "gy", None),
        P("gx", "gy"),
    )
    return jax.shard_map(
        on_device,
        mesh=mesh,
        in_specs=placed,
        out_specs=P("gx", "gy", None, None, None),
        check_vma=False,
    )
```
